512 devices in a mesh: dp: 8 (over y), fsdp: 64 (over x, z, core).
Axes of the slice: x: 4, y: 8, z: 8, core: 2. Of those that a mesh axis runs over, the one named last changes fastest.
Arguments:
- q_pre: bfloat16 [8, 8192, 3072], P('dp', 'fsdp'), may hold values from -8 to 8
- k_pre: bfloat16 [8, 8192, 3072], P('dp', 'fsdp'), may hold values from -8 to 8
- values: bfloat16 [8, 8192, 3072], P('dp', 'fsdp'), may hold values from -6 to 6
- grad_out: bfloat16 [8, 8192, 3072], P('dp', 'fsdp'), may hold values from -6 to 6
- segment_ids: int32 [8, 8192], P('dp', 'fsdp'), may hold values from 0 to 127, never falling along the last dimension, each value on 1 to 128 neighbouring positions
- gain_q: float32 [24, 128], replicated, may hold values from 0.5 to 4.5
- gain_k: float32 [24, 128], replicated, may hold values from 0.5 to 4.5
Outputs:
- grad_q_pre: bfloat16 [8, 8192, 3072], P('dp', 'fsdp')
- grad_k_pre: bfloat16 [8, 8192, 3072], P('dp', 'fsdp')
- grad_gain_q: float32 [24, 128], replicated
- grad_gain_k: float32 [24, 128], replicated
The draws below stay inside these ranges and needn't reach their ends.
Inputs may be any that keep to these rules, and one draw needn't show every extreme that they name: `segment_ids`: in each group, ids never fall along the positions; every image covers 1 to 128 positions, and one covers exactly 128.
All inputs are finite; a program needn't handle non-finite values.
Results may differ from the reference program's by a relative error of at most 0.011.
The reference program's roundings to bfloat16 on the way (of `slopes`) count: a program that leaves them out, or rounds other values in their place, can miss the bound.
Values may be sent and summed in bfloat16 or wider, within the bound.
A program may use at most 64 MiB of HBM per device.

```python
import math
import jax
import jax.numpy as jnp
import numpy as np
from jax import lax

HEADS = 24
DEPTH = 128
TOK_DEV = 128
GROUPS = 8
TOKENS = 8192
IMAGES = 128


def shared_keys(key):
    base = jax.random.normal(jax.random.fold_in(key, 17), (GROUPS, TOKENS, HEADS * DEPTH), jnp.float32)
    noise = jax.random.normal(jax.random.fold_in(key, 19), (GROUPS, TOKENS, HEADS * DEPTH), jnp.float32)
    return jnp.clip(1.2 * base + 0.6 * noise, -8.0, 8.0)


def draw_k_pre(key, part):
    full = shared_keys(key)
    return full.astype(jnp.bfloat16)


def draw_q_pre(key, part):
    key = jax.random.fold_in(key, 5)
    own = jnp.clip(1.3 * jax.random.normal(key, (GROUPS, TOKENS, HEADS * DEPTH), jnp.float32), -8.0, 8.0)
    return own.astype(jnp.bfloat16)


def draw_gain_q(key, part):
    key = jax.random.fold_in(key, 7)
    return jax.random.uniform(key, (HEADS, DEPTH), jnp.float32, 0.6, 1.6)


def draw_gain_k(key, part):
    key = jax.random.fold_in(key, 9)
    return jax.random.uniform(key, (HEADS, DEPTH), jnp.float32, 0.6, 1.6)


def block_levels(stream_key, shape, pieces, least, largest):
    def one(dim, parts):
        heights = jax.random.uniform(jax.random.fold_in(jax.random.fold_in(stream_key, 6), dim), (parts,), jnp.float32, least / len(pieces), largest / len(pieces))
        return jnp.repeat(jnp.exp(heights), shape[dim] // parts).reshape((-1,) + (1,) * (len(shape) - dim - 1))

    level = one(*pieces[0])
    for cut in pieces[1:]:
        level = level * one(*cut)
    return level


def length_profile(count, total, limit, lean):
    loads = [(1 << 20) // math.isqrt(grade ** lean) + 1 for grade in range(2, count + 1)]
    surplus, holding = total - limit - (count - 1), [1] * (count - 1)
    while surplus > 0:
        candidates = [i for i in range(count - 1) if holding[i] < limit]
        whole, budget = sum([loads[i] for i in candidates]), surplus
        for i in candidates:
            more = min(limit - holding[i], max(1, budget * loads[i] // whole), surplus)
            holding[i] = holding[i] + more
            surplus = surplus - more
    return np.array([limit] + holding)


def uneven_parts(key, count, total, bound, skew):
    if count == 2:
        one = jax.random.randint(key, (), max(1, total - bound), min(bound, total - 1) + 1)
        return jnp.stack([one, total - one])
    tallies = jnp.asarray(length_profile(count, total, bound, skew), jnp.int32)
    pairs = (count - 1) // 2
    source_of, receiver = tallies[1:1 + 2 * pairs:2], tallies[2:2 + 2 * pairs:2]
    room = jnp.minimum(source_of - 1, bound - receiver)
    passed = jax.random.randint(jax.random.fold_in(key, 1), (pairs,), 0, 1 << 20) % (room + 1)
    tallies = tallies.at[1:1 + 2 * pairs:2].set(source_of - passed).at[2:2 + 2 * pairs:2].set(receiver + passed)
    return tallies[jax.random.permutation(jax.random.fold_in(key, 2), count)]


def centred(rng, extent, spread, reach, split=(), kind=jnp.bfloat16):
    entries = jax.random.normal(rng, extent, jnp.float32) * spread
    if len(split) > 0:
        entries = block_levels(rng, extent, split, -0.22, 0.18) * entries
    return jnp.clip(entries, min=-reach, max=reach).astype(kind)


def setup_inputs(seed: int = 0) -> dict:
    arg_keys = jax.random.split(jax.random.key(seed), 8)
    q_pre = draw_q_pre(jax.random.fold_in(arg_keys[7], 71), 0)
    k_pre = draw_k_pre(jax.random.fold_in(arg_keys[7], 71), 0)
    values = centred(arg_keys[2], (GROUPS, TOKENS, HEADS * DEPTH), 1.0, 6.0, ((0, 8), (1, 64)))
    grad_out = centred(arg_keys[3], (GROUPS, TOKENS, HEADS * DEPTH), 1.0, 6.0, ((0, 8), (1, 64)))
    segment_ids = jax.vmap(lambda own: jnp.searchsorted(jnp.cumsum(uneven_parts(own, IMAGES, TOKENS, TOK_DEV, 2)), jnp.arange(TOKENS), side="right"))(jax.random.split(arg_keys[4], GROUPS)).reshape((GROUPS, TOKENS)).astype(jnp.int32)
    gain_q = draw_gain_q(jax.random.fold_in(arg_keys[7], 71), 0)
    gain_k = draw_gain_k(jax.random.fold_in(arg_keys[7], 71), 0)
    return dict(q_pre=q_pre, k_pre=k_pre, values=values, grad_out=grad_out, segment_ids=segment_ids, gain_q=gain_q, gain_k=gain_k)


def layer_norm(x, gain):
    mean = lax.optimization_barrier(jnp.mean(x, -1, keepdims=True))
    centered = x - mean
    var = lax.optimization_barrier(jnp.mean(centered * centered, -1, keepdims=True))
    return centered * lax.rsqrt(var + 1e-06) * gain

def softmax_grads(queries, cotangent, keys, values, query_ids, key_ids, scale):
    scores = jnp.einsum('qhd,khd->hqk', queries.astype(jnp.float32), keys.astype(jnp.float32)) * scale
    match = (query_ids[:, None] == key_ids[None, :])[None]
    masked = jnp.where(match, scores, jnp.float32(-1e+30))
    top = lax.optimization_barrier(jnp.max(masked, -1, keepdims=True))
    expo = jnp.where(match, jnp.exp(masked - top), jnp.float32(0.0))
    total = lax.optimization_barrier(jnp.sum(expo, -1, keepdims=True))
    probs = expo / total
    dprob = jnp.einsum('qhd,khd->hqk', cotangent.astype(jnp.float32), values.astype(jnp.float32))
    delta = lax.optimization_barrier(jnp.sum(probs * dprob, -1, keepdims=True))
    slopes = (probs * (dprob - delta) * scale).astype(jnp.bfloat16)
    return slopes

def group_grads(q_pre, k_pre, values, grad_out, ids, gain_q, gain_k):
    heads, depth = gain_q.shape
    tokens = q_pre.shape[0]
    rows = TOK_DEV
    scale = depth ** (-0.5)
    q_float = q_pre.astype(jnp.float32).reshape(tokens, heads, depth)
    k_float = k_pre.astype(jnp.float32).reshape(tokens, heads, depth)
    q_normed, q_back = jax.vjp(layer_norm, q_float, gain_q)
    k_normed, k_back = jax.vjp(layer_norm, k_float, gain_k)
    queries = q_normed.astype(jnp.bfloat16)
    keys = k_normed.astype(jnp.bfloat16)
    vals = values.reshape(tokens, heads, depth)
    cotan = grad_out.reshape(tokens, heads, depth)
    seg = ids + 1
    edge = rows
    keys_pad = jnp.pad(keys, ((edge, edge), (0, 0), (0, 0)))
    vals_pad = jnp.pad(vals, ((edge, edge), (0, 0), (0, 0)))
    seg_pad = jnp.pad(seg, (edge, edge))

    def block(carry, index):
        start = (index * rows).astype(jnp.int32)
        q_blk = lax.dynamic_slice_in_dim(queries, start, rows, 0)
        c_blk = lax.dynamic_slice_in_dim(cotan, start, rows, 0)
        s_blk = lax.dynamic_slice_in_dim(seg, start, rows, 0)
        k_win = lax.dynamic_slice_in_dim(keys_pad, start, 3 * rows, 0)
        v_win = lax.dynamic_slice_in_dim(vals_pad, start, 3 * rows, 0)
        s_win = lax.dynamic_slice_in_dim(seg_pad, start, 3 * rows, 0)
        slopes = softmax_grads(q_blk, c_blk, k_win, v_win, s_blk, s_win, scale)
        dq_blk = jnp.einsum('hqk,khd->qhd', slopes.astype(jnp.float32), k_win.astype(jnp.float32))
        dk_win = jnp.einsum('hqk,qhd->khd', slopes.astype(jnp.float32), q_blk.astype(jnp.float32))
        current = lax.dynamic_slice_in_dim(carry, start, 3 * rows, 0)
        carry = lax.dynamic_update_slice_in_dim(carry, current + dk_win, start, 0)
        return (carry, dq_blk)
    carry0 = jnp.zeros((tokens + 2 * edge, heads, depth), jnp.float32)
    carry, dq_blocks = lax.scan(block, carry0, jnp.arange(tokens // rows, dtype=jnp.int32))
    grad_q = dq_blocks.reshape(tokens, heads, depth)
    grad_k = carry[edge:edge + tokens]
    dq_pre, dgain_q = q_back(grad_q)
    dk_pre, dgain_k = k_back(grad_k)
    width = heads * depth
    return (dq_pre.reshape(tokens, width).astype(jnp.bfloat16), dk_pre.reshape(tokens, width).astype(jnp.bfloat16), dgain_q, dgain_k)

def reference(q_pre, k_pre, values, grad_out, segment_ids, gain_q, gain_k):

    def one_group(items):
        return group_grads(items[0], items[1], items[2], items[3], items[4], gain_q, gain_k)
    outs = lax.map(one_group, (q_pre, k_pre, values, grad_out, segment_ids))
    return (outs[0], outs[1], lax.optimization_barrier(jnp.sum(outs[2], 0)), lax.optimization_barrier(jnp.sum(outs[3], 0)))
```

```python
import math

import jax
import jax.numpy as jnp
from jax import lax
from jax.experimental import pallas as pl
from jax.experimental.pallas import tpu as pltpu
from jax.sharding import PartitionSpec as P

MESH = pl.DeviceIdType.MESH
F32 = jnp.float32
BF16 = jnp.bfloat16

HEADS = 24
DEPTH = 128
ROWS = 128
HALF = ROWS // 2
WIDTH = HEADS * DEPTH
PER_STEP = 2
STEPS = HEADS // PER_STEP
COLS = PER_STEP * DEPTH
SCALE = DEPTH**-0.5
SCALE_LOG2 = SCALE * math.log2(math.e)


def dot(a, b, contract_a, contract_b):
    dims = (((contract_a,), (contract_b,)), ((), ()))
    return lax.dot_general(a, b, dims, preferred_element_type=F32)


def lane_mean(x):
    return jnp.sum(x, -1, keepdims=True) * (1.0 / DEPTH)


def normalize(x, gain):
    centered = x - lane_mean(x)
    inverse = lax.rsqrt(lane_mean(centered * centered) + 1e-06)
    unit = centered * inverse
    return unit, inverse, (unit * gain).astype(BF16)


def normalize_back(grad, unit, inverse, gain):
    d_unit = grad * gain
    mean = lane_mean(d_unit)
    slope = lane_mean(d_unit * unit)
    return (inverse * (d_unit - mean - unit * slope)).astype(BF16)


def attention_back(queries, keys, values, cotangent, bias):
    scores = dot(keys, queries, 1, 1) * SCALE_LOG2 + bias
    expo = jnp.exp2(scores - jnp.max(scores, 0, keepdims=True))
    total = jnp.sum(expo, 0, keepdims=True)
    dprob = dot(values, cotangent, 1, 1)
    delta = jnp.sum(expo * dprob, 0, keepdims=True) / total
    slopes = (expo * (SCALE / total) * (dprob - delta)).astype(BF16)
    return dot(slopes, keys, 0, 0), dot(slopes, queries, 1, 0)


def place():
    f = lax.axis_index("fsdp")
    return lax.axis_index("dp"), f // 16, lax.rem(f, 16) // 2, lax.rem(f, 2)


def groups():
    y, x, z, c = place()
    return {
        "core": (2, c, lambda j: {"fsdp": x * 16 + z * 2 + j}),
        "x": (4, x, lambda j: {"fsdp": j * 16 + z * 2 + c}),
        "y": (8, y, lambda j: {"dp": j}),
        "z": (8, z, lambda j: {"fsdp": x * 16 + j * 2 + c}),
    }


def greet(left, right):
    barrier = pltpu.get_barrier_semaphore()
    for device in (left, right):
        pl.semaphore_signal(barrier, inc=1, device_id=device, device_id_type=MESH)
    count = 2
    for size, me, member in groups().values():
        for i in range(1, size):
            peer = member(lax.rem(me + i, size))
            pl.semaphore_signal(barrier, inc=1, device_id=peer, device_id_type=MESH)
        count += size - 1
    return barrier, count


def kernel(
    q_ref, k_ref, v_ref, g_ref, ids_ref, gain_q_ref, gain_k_ref,
    out_q_ref, out_k_ref, sum_ref,
    own, halo, sent_back, came_back, result, gains, d_gains,
    ids_in, ids_own, ids_near, bias, weight, given,
    core_in, x_in, y_in, z_in, final,
    local_sem, id_send, id_recv, far_send, far_recv, back_send, back_recv,
    core_sem, x_sem, y_sem, z_sem, last_sem,
):
    f = lax.axis_index("fsdp")
    size = lax.axis_size("fsdp")
    left = {"fsdp": lax.rem(f + size - 1, size)}
    right = {"fsdp": lax.rem(f + 1, size)}
    barrier, count = greet(left, right)

    sources = (q_ref, k_ref, v_ref, g_ref)
    loads = [pltpu.make_async_copy(ids_ref, ids_in, local_sem.at[4])]
    loads += [pltpu.make_async_copy(s, own.at[i], local_sem.at[i]) for i, s in enumerate(sources)]
    loads += [
        pltpu.make_async_copy(gain_q_ref, gains.at[0], local_sem.at[5]),
        pltpu.make_async_copy(gain_k_ref, gains.at[1], local_sem.at[6]),
    ]
    for load in loads:
        load.start()
    loads[0].wait()
    ids_own[...] = jnp.broadcast_to(ids_in[...], (8, ROWS))
    pl.semaphore_wait(barrier, count)

    def id_copy(side):
        return pltpu.make_async_remote_copy(
            src_ref=ids_own, dst_ref=ids_near.at[side], send_sem=id_send.at[side], recv_sem=id_recv.at[side],
            device_id=(left, right)[side], device_id_type=MESH,
        )

    def far_copy(step, array, side):
        rows = pl.ds(side * HALF, HALF)
        columns = pl.ds(pl.multiple_of(step * COLS, COLS), COLS)
        return pltpu.make_async_remote_copy(
            src_ref=sources[array].at[rows, columns], dst_ref=halo.at[array, rows, columns],
            send_sem=far_send.at[side, array, step], recv_sem=far_recv.at[side, array, step],
            device_id=(left, right)[side], device_id_type=MESH,
        )

    def back_copy(step, array, side):
        rows = pl.ds(side * HALF, HALF)
        columns = pl.ds(pl.multiple_of(step * COLS, COLS), COLS)
        return pltpu.make_async_remote_copy(
            src_ref=sent_back.at[array, rows, columns], dst_ref=came_back.at[array, rows, columns],
            send_sem=back_send.at[side, array, step], recv_sem=back_recv.at[side, array, step],
            device_id=(right, left)[side], device_id_type=MESH,
        )

    for side in (0, 1):
        id_copy(side).start()

    def send_far(step, carry):
        for array in range(4):
            for side in (0, 1):
                far_copy(step, array, side).start()
        return carry

    lax.fori_loop(0, STEPS, send_far, 0)

    for side in (0, 1):
        id_copy(side).wait()
    mine = ids_own[0:1, :]
    after = jnp.where(f < size - 1, ids_near[0, 0:1, :], -2)
    before = jnp.where(f > 0, ids_near[1, 0:1, :], -2)
    lane = lax.broadcasted_iota(jnp.int32, (1, ROWS), 1)

    def pick(x, at):
        return jnp.sum(jnp.where(lane == at, x, 0), -1, keepdims=True)

    first, last = pick(mine, 0), pick(mine, ROWS - 1)
    tail_before, head_after = pick(before, ROWS - 1), pick(after, 0)
    half_before, half_mine = pick(before, HALF - 1), pick(mine, HALF - 1)
    in_left = mine == tail_before
    in_right = mine == head_after
    take_left = half_before != first
    take_right = half_mine == last
    low = lane < HALF
    use_right = low & (after == last) & take_right
    use_left = (~low) & (before == first) & take_left
    halo_ids = jnp.where(use_right | use_left, jnp.where(low, after, before), -1)
    given_row = ((in_left & ~take_left) | (in_right & ~take_right)).astype(F32)
    used_row = (use_right | use_left).astype(F32)
    ids_row = jnp.concatenate([mine, halo_ids], 1).astype(F32)
    across = jnp.broadcast_to(ids_row, (2 * ROWS, 2 * ROWS))
    bias[...] = jnp.where(across == across.T, 0.0, -1e30).astype(F32)
    weight_row = jnp.concatenate([1.0 - given_row, used_row], 1)
    weight[...] = jnp.broadcast_to(weight_row, (ROWS, 2 * ROWS)).T
    given[...] = jnp.broadcast_to(given_row, (ROWS, ROWS)).T

    for load in loads[1:]:
        load.wait()

    def compute(step, carry):
        for array in range(4):
            for side in (0, 1):
                far_copy(step, array, side).wait_recv()
        for part in range(PER_STEP):
            head = step * PER_STEP + part
            columns = pl.ds(pl.multiple_of(head * DEPTH, DEPTH), DEPTH)
            gain = [gains[i, pl.ds(head, 1), :] for i in range(2)]
            raw = [jnp.concatenate([own[i, :, columns], halo[i, :, columns]], 0) for i in range(4)]
            unit, inverse, normed = zip(*[normalize(raw[i].astype(F32), gain[i]) for i in range(2)])
            grads = attention_back(normed[0], normed[1], raw[2], raw[3], bias[...])
            for i in range(2):
                d_gains[i, pl.ds(head, 1), :] = jnp.sum(grads[i] * unit[i] * weight[...], 0, keepdims=True)
                d_raw = normalize_back(grads[i], unit[i], inverse[i], gain[i])
                result[i, :, columns] = d_raw[:ROWS]
                sent_back[i, :, columns] = d_raw[ROWS:]
        return carry

    lax.fori_loop(0, STEPS, compute, 0)

    def send_back(step, carry):
        for array in range(2):
            for side in (0, 1):
                back_copy(step, array, side).start()
        return carry

    lax.fori_loop(0, STEPS, send_back, 0)

    members = groups()
    core = members["core"][1]
    other = 1 - core

    def core_copy(source, target, pair):
        return pltpu.make_async_remote_copy(
            src_ref=source, dst_ref=target, send_sem=pair.at[0], recv_sem=pair.at[1],
            device_id=members["core"][2](other), device_id_type=MESH,
        )

    first_copy = core_copy(d_gains.at[other], core_in, core_sem)
    first_copy.start()
    first_copy.wait()

    def exchange(name, block, slots, sems):
        size, me, member = members[name]
        slots[me] = block
        copies = []
        for i in range(1, size):
            peer = lax.rem(me + i, size)
            copies.append(
                pltpu.make_async_remote_copy(
                    src_ref=slots.at[me], dst_ref=slots.at[me], send_sem=sems.at[0, i], recv_sem=sems.at[1, size - i],
                    device_id=member(peer), device_id_type=MESH,
                )
            )
        for copy in copies:
            copy.start()
        return copies

    def total(slots, copies):
        for copy in copies:
            copy.wait()
        return jnp.sum(slots[...], 0)

    copies = exchange("x", d_gains[core] + core_in[...], x_in, x_sem)
    copies = exchange("y", total(x_in, copies), y_in, y_sem)
    copies = exchange("z", total(y_in, copies), z_in, z_sem)

    def finish(step, carry):
        for array in range(2):
            for side in (0, 1):
                back_copy(step, array, side).wait_recv()
        for part in range(PER_STEP):
            columns = pl.ds(pl.multiple_of(step * COLS + part * DEPTH, DEPTH), DEPTH)
            away = given[...] != 0.0
            for i in range(2):
                mixed = jnp.where(away, came_back[i, :, columns].astype(F32), result[i, :, columns].astype(F32))
                result[i, :, columns] = mixed.astype(BF16)
        return carry

    lax.fori_loop(0, STEPS, finish, 0)
    stores = [
        pltpu.make_async_copy(result.at[i], out, local_sem.at[i]) for i, out in enumerate((out_q_ref, out_k_ref))
    ]
    for store in stores:
        store.start()
    final[core] = total(z_in, copies)
    last_copy = core_copy(final.at[core], final.at[core], last_sem)
    last_copy.start()
    last_copy.wait()
    sum_ref[...] = final[...]

    def drain(step, carry):
        for side in (0, 1):
            for array in range(4):
                far_copy(step, array, side).wait_send()
            for array in range(2):
                back_copy(step, array, side).wait_send()
        return carry

    lax.fori_loop(0, STEPS, drain, 0)
    for store in stores:
        store.wait()


def per_device(q_pre, k_pre, values, grad_out, segment_ids, gain_q, gain_k):
    anywhere = pl.BlockSpec(memory_space=pl.ANY)
    vmem, dma = pltpu.VMEM, pltpu.SemaphoreType.DMA
    wide = (ROWS, WIDTH)
    part = (HEADS, DEPTH)
    out_q, out_k, sums = pl.pallas_call(
        kernel,
        out_shape=[
            jax.ShapeDtypeStruct(wide, BF16),
            jax.ShapeDtypeStruct(wide, BF16),
            jax.ShapeDtypeStruct((2,) + part, F32),
        ],
        in_specs=[anywhere] * 7,
        out_specs=[anywhere, anywhere, pl.BlockSpec(memory_space=vmem)],
        scratch_shapes=[
            vmem((4,) + wide, BF16),
            vmem((4,) + wide, BF16),
            vmem((2,) + wide, BF16),
            vmem((2,) + wide, BF16),
            vmem((2,) + wide, BF16),
            vmem((2,) + part, F32),
            vmem((2,) + part, F32),
            vmem((1, ROWS), jnp.int32),
            vmem((8, ROWS), jnp.int32),
            vmem((2, 8, ROWS), jnp.int32),
            vmem((2 * ROWS, 2 * ROWS), F32),
            vmem((2 * ROWS, ROWS), F32),
            vmem((ROWS, ROWS), F32),
            vmem(part, F32),
            vmem((4,) + part, F32),
            vmem((8,) + part, F32),
            vmem((8,) + part, F32),
            vmem((2,) + part, F32),
            dma((7,)),
            dma((2,)),
            dma((2,)),
            dma((2, 4, STEPS)),
            dma((2, 4, STEPS)),
            dma((2, 2, STEPS)),
            dma((2, 2, STEPS)),
            dma((2,)),
            dma((2, 4)),
            dma((2, 8)),
            dma((2, 8)),
            dma((2,)),
        ],
        compiler_params=pltpu.CompilerParams(
            collective_id=0, has_side_effects=True, vmem_limit_bytes=56 * 1024 * 1024
        ),
        cost_estimate=pl.CostEstimate(
            flops=HEADS * 8 * 256 * 256 * 128, bytes_accessed=5 << 20, transcendentals=HEADS * 256 * 256
        ),
    )(q_pre[0], k_pre[0], values[0], grad_out[0], segment_ids, gain_q, gain_k)
    return out_q[None], out_k[None], sums[0], sums[1]


def solution(mesh):
    tokens = P("dp", "fsdp", None)
    return jax.shard_map(
        per_device,
        mesh=mesh,
        in_specs=(tokens, tokens, tokens, tokens, P("dp", "fsdp"), P(), P()),
        out_specs=(tokens, tokens, P(), P()),
        check_vma=False,
    )
```

```python
import math

import jax
import jax.numpy as jnp
from jax import lax
from jax.experimental import pallas as pl
from jax.experimental.pallas import tpu as pltpu
from jax.sharding import PartitionSpec as P

MESH = pl.DeviceIdType.MESH
F32 = jnp.float32
BF16 = jnp.bfloat16

HEADS = 24
DEPTH = 128
ROWS = 128
HALF = ROWS // 2
WIDTH = HEADS * DEPTH
PER_STEP = 2
STEPS = HEADS // PER_STEP
COLS = PER_STEP * DEPTH
SCALE = DEPTH**-0.5
SCALE_LOG2 = SCALE * math.log2(math.e)


def dot(a, b, contract_a, contract_b):
    dims = (((contract_a,), (contract_b,)), ((), ()))
    return lax.dot_general(a, b, dims, preferred_element_type=F32)


def lane_mean(x):
    return jnp.sum(x, -1, keepdims=True) * (1.0 / DEPTH)


def normalize(x, gain):
    centered = x - lane_mean(x)
    inverse = lax.rsqrt(lane_mean(centered * centered) + 1e-06)
    unit = centered * inverse
    return unit, inverse, (unit * gain).astype(BF16)


def normalize_back(grad, unit, inverse, gain):
    d_unit = grad * gain
    mean = lane_mean(d_unit)
    slope = lane_mean(d_unit * unit)
    return (inverse * (d_unit - mean - unit * slope)).astype(BF16)


def attention_back(queries, keys, values, cotangent, bias):
    scores = dot(keys, queries, 1, 1) * SCALE_LOG2 + bias
    expo = jnp.exp2(scores - jnp.max(scores, 0, keepdims=True))
    total = jnp.sum(expo, 0, keepdims=True)
    dprob = dot(values, cotangent, 1, 1)
    delta = jnp.sum(expo * dprob, 0, keepdims=True) / total
    slopes = (expo * (SCALE / total) * (dprob - delta)).astype(BF16)
    return dot(slopes, keys, 0, 0), dot(slopes, queries, 1, 0)


def place():
    f = lax.axis_index("fsdp")
    return lax.axis_index("dp"), f // 16, lax.rem(f, 16) // 2, lax.rem(f, 2)


def groups():
    y, x, z, c = place()
    return {
        "core": (2, c, lambda j: {"fsdp": x * 16 + z * 2 + j}),
        "x": (4, x, lambda j: {"fsdp": j * 16 + z * 2 + c}),
        "y": (8, y, lambda j: {"dp": j}),
        "z": (8, z, lambda j: {"fsdp": x * 16 + j * 2 + c}),
    }


def signal_around(sem, axes, distance):
    for name in axes:
        size, me, member = groups()[name]
        for step in (distance, size - distance):
            peer = member(lax.rem(me + step, size))
            pl.semaphore_signal(sem, inc=1, device_id=peer, device_id_type=MESH)
    return 2 * len(axes)


def kernel(
    q_ref, k_ref, v_ref, g_ref, ids_ref, gain_q_ref, gain_k_ref,
    result, sum_ref,
    own, halo, sent_back, came_back, gains, d_gains,
    ids_in, ids_own, ids_near, bias, weight, given,
    core_in, x_in, y_in, z_in, final,
    local_sem, id_send, id_recv, far_send, far_recv, back_send, back_recv,
    core_sem, x_sem, y_sem, z_sem, last_sem, heard_1, heard_2,
):
    f = lax.axis_index("fsdp")
    size = lax.axis_size("fsdp")
    left = {"fsdp": lax.rem(f + size - 1, size)}
    right = {"fsdp": lax.rem(f + 1, size)}
    barrier = pltpu.get_barrier_semaphore()
    for device in (left, right):
        pl.semaphore_signal(barrier, inc=1, device_id=device, device_id_type=MESH)
    count = 2 + signal_around(barrier, "xyz", 1)

    sources = (q_ref, k_ref, v_ref, g_ref)
    loads = [pltpu.make_async_copy(ids_ref, ids_in, local_sem.at[4])]
    loads += [pltpu.make_async_copy(s, own.at[i], local_sem.at[i]) for i, s in enumerate(sources)]
    loads += [
        pltpu.make_async_copy(gain_q_ref, gains.at[0], local_sem.at[5]),
        pltpu.make_async_copy(gain_k_ref, gains.at[1], local_sem.at[6]),
    ]
    for load in loads:
        load.start()
    loads[0].wait()
    ids_own[...] = jnp.broadcast_to(ids_in[...], (8, ROWS))
    pl.semaphore_wait(barrier, count)

    def id_copy(side):
        return pltpu.make_async_remote_copy(
            src_ref=ids_own, dst_ref=ids_near.at[side], send_sem=id_send.at[side], recv_sem=id_recv.at[side],
            device_id=(left, right)[side], device_id_type=MESH,
        )

    def far_copy(step, array, side):
        rows = pl.ds(side * HALF, HALF)
        columns = pl.ds(pl.multiple_of(step * COLS, COLS), COLS)
        return pltpu.make_async_remote_copy(
            src_ref=sources[array].at[rows, columns], dst_ref=halo.at[array, rows, columns],
            send_sem=far_send.at[side, array, step], recv_sem=far_recv.at[side, array, step],
            device_id=(left, right)[side], device_id_type=MESH,
        )

    def back_copy(step, array, side):
        rows = pl.ds(side * HALF, HALF)
        columns = pl.ds(pl.multiple_of(step * COLS, COLS), COLS)
        return pltpu.make_async_remote_copy(
            src_ref=sent_back.at[array, rows, columns], dst_ref=came_back.at[array, rows, columns],
            send_sem=back_send.at[side, array, step], recv_sem=back_recv.at[side, array, step],
            device_id=(right, left)[side], device_id_type=MESH,
        )

    for side in (0, 1):
        id_copy(side).start()

    def send_far(step, carry):
        for array in range(4):
            for side in (0, 1):
                far_copy(step, array, side).start()
        return carry

    lax.fori_loop(0, STEPS, send_far, 0)
    near = signal_around(heard_1, "xyz", 1)

    for side in (0, 1):
        id_copy(side).wait()
    mine = ids_own[0:1, :]
    after = jnp.where(f < size - 1, ids_near[0, 0:1, :], -2)
    before = jnp.where(f > 0, ids_near[1, 0:1, :], -2)
    lane = lax.broadcasted_iota(jnp.int32, (1, ROWS), 1)

    def pick(x, at):
        return jnp.sum(jnp.where(lane == at, x, 0), -1, keepdims=True)

    first, last = pick(mine, 0), pick(mine, ROWS - 1)
    tail_before, head_after = pick(before, ROWS - 1), pick(after, 0)
    half_before, half_mine = pick(before, HALF - 1), pick(mine, HALF - 1)
    in_left = mine == tail_before
    in_right = mine == head_after
    take_left = half_before != first
    take_right = half_mine == last
    low = lane < HALF
    use_right = low & (after == last) & take_right
    use_left = (~low) & (before == first) & take_left
    halo_ids = jnp.where(use_right | use_left, jnp.where(low, after, before), -1)
    given_row = ((in_left & ~take_left) | (in_right & ~take_right)).astype(F32)
    used_row = (use_right | use_left).astype(F32)
    ids_row = jnp.concatenate([mine, halo_ids], 1).astype(F32)
    across = jnp.broadcast_to(ids_row, (2 * ROWS, 2 * ROWS))
    bias[...] = jnp.where(across == across.T, 0.0, -1e30).astype(F32)
    weight_row = jnp.concatenate([1.0 - given_row, used_row], 1)
    weight[...] = jnp.broadcast_to(weight_row, (ROWS, 2 * ROWS)).T
    given[...] = jnp.broadcast_to(given_row, (ROWS, ROWS)).T

    pl.semaphore_wait(heard_1, near)
    next_near = signal_around(heard_2, "yz", 2)
    for load in loads[1:]:
        load.wait()

    def compute(step, carry):
        for array in range(4):
            for side in (0, 1):
                far_copy(step, array, side).wait_recv()
        for part in range(PER_STEP):
            head = step * PER_STEP + part
            columns = pl.ds(pl.multiple_of(head * DEPTH, DEPTH), DEPTH)
            gain = [gains[i, pl.ds(head, 1), :] for i in range(2)]
            raw = [jnp.concatenate([own[i, :, columns], halo[i, :, columns]], 0) for i in range(4)]
            unit, inverse, normed = zip(*[normalize(raw[i].astype(F32), gain[i]) for i in range(2)])
            grads = attention_back(normed[0], normed[1], raw[2], raw[3], bias[...])
            for i in range(2):
                d_gains[i, pl.ds(head, 1), :] = jnp.sum(grads[i] * unit[i] * weight[...], 0, keepdims=True)
                d_raw = normalize_back(grads[i], unit[i], inverse[i], gain[i])
                result[i, :, columns] = d_raw[:ROWS]
                sent_back[i, :, columns] = d_raw[ROWS:]
        for array in range(2):
            for side in (0, 1):
                back_copy(step, array, side).start()
        return carry

    lax.fori_loop(0, STEPS, compute, 0)

    pl.semaphore_wait(heard_2, next_near)
    members = groups()
    core = members["core"][1]
    other = 1 - core

    def core_copy(source, target, pair):
        return pltpu.make_async_remote_copy(
            src_ref=source, dst_ref=target, send_sem=pair.at[0], recv_sem=pair.at[1],
            device_id=members["core"][2](other), device_id_type=MESH,
        )

    first_copy = core_copy(d_gains.at[other], core_in, core_sem)
    first_copy.start()
    first_copy.wait()

    def exchange(name, block, slots, sems):
        size, me, member = members[name]
        slots[me] = block
        copies = []
        for i in range(1, size):
            peer = lax.rem(me + i, size)
            copies.append(
                pltpu.make_async_remote_copy(
                    src_ref=slots.at[me], dst_ref=slots.at[me], send_sem=sems.at[0, i], recv_sem=sems.at[1, size - i],
                    device_id=member(peer), device_id_type=MESH,
                )
            )
        for copy in copies:
            copy.start()
        return copies

    def total(slots, copies):
        for copy in copies:
            copy.wait()
        return jnp.sum(slots[...], 0)

    copies = exchange("x", d_gains[core] + core_in[...], x_in, x_sem)
    copies = exchange("y", total(x_in, copies), y_in, y_sem)
    copies = exchange("z", total(y_in, copies), z_in, z_sem)

    def finish(step, carry):
        for array in range(2):
            for side in (0, 1):
                back_copy(step, array, side).wait_recv()
        for part in range(PER_STEP):
            columns = pl.ds(pl.multiple_of(step * COLS + part * DEPTH, DEPTH), DEPTH)
            away = given[...] != 0.0
            for i in range(2):
                mixed = jnp.where(away, came_back[i, :, columns].astype(F32), result[i, :, columns].astype(F32))
                result[i, :, columns] = mixed.astype(BF16)
        return carry

    lax.fori_loop(0, STEPS, finish, 0)
    final[core] = total(z_in, copies)
    last_copy = core_copy(final.at[core], final.at[core], last_sem)
    last_copy.start()
    last_copy.wait()
    sum_ref[...] = final[...]

    def drain(step, carry):
        for side in (0, 1):
            for array in range(4):
                far_copy(step, array, side).wait_send()
            for array in range(2):
                back_copy(step, array, side).wait_send()
        return carry

    lax.fori_loop(0, STEPS, drain, 0)


def hand_out(result, sums, out_q, out_k, sum_q, sum_k, sem):
    copies = [pltpu.make_async_copy(result.at[i], out, sem.at[i]) for i, out in enumerate((out_q, out_k))]
    copies += [pltpu.make_async_copy(sums.at[i], out, sem.at[2 + i]) for i, out in enumerate((sum_q, sum_k))]
    for copy in copies:
        copy.start()
    for copy in copies:
        copy.wait()


def per_device(q_pre, k_pre, values, grad_out, segment_ids, gain_q, gain_k):
    anywhere = pl.BlockSpec(memory_space=pl.ANY)
    vmem, dma = pltpu.VMEM, pltpu.SemaphoreType.DMA
    wide = (ROWS, WIDTH)
    part = (HEADS, DEPTH)
    result, sums = pl.pallas_call(
        kernel,
        out_shape=[vmem((2,) + wide, BF16), vmem((2,) + part, F32)],
        in_specs=[anywhere] * 7,
        out_specs=[pl.BlockSpec(memory_space=vmem)] * 2,
        scratch_shapes=[
            vmem((4,) + wide, BF16),
            vmem((4,) + wide, BF16),
            vmem((2,) + wide, BF16),
            vmem((2,) + wide, BF16),
            vmem((2,) + part, F32),
            vmem((2,) + part, F32),
            vmem((1, ROWS), jnp.int32),
            vmem((8, ROWS), jnp.int32),
            vmem((2, 8, ROWS), jnp.int32),
            vmem((2 * ROWS, 2 * ROWS), F32),
            vmem((2 * ROWS, ROWS), F32),
            vmem((ROWS, ROWS), F32),
            vmem(part, F32),
            vmem((4,) + part, F32),
            vmem((8,) + part, F32),
            vmem((8,) + part, F32),
            vmem((2,) + part, F32),
            dma((7,)),
            dma((2,)),
            dma((2,)),
            dma((2, 4, STEPS)),
            dma((2, 4, STEPS)),
            dma((2, 2, STEPS)),
            dma((2, 2, STEPS)),
            dma((2,)),
            dma((2, 4)),
            dma((2, 8)),
            dma((2, 8)),
            dma((2,)),
            pltpu.SemaphoreType.REGULAR,
            pltpu.SemaphoreType.REGULAR,
        ],
        compiler_params=pltpu.CompilerParams(
            collective_id=0, has_side_effects=True, vmem_limit_bytes=56 * 1024 * 1024
        ),
        cost_estimate=pl.CostEstimate(
            flops=HEADS * 8 * 256 * 256 * 128, bytes_accessed=5 << 20, transcendentals=HEADS * 256 * 256
        ),
    )(q_pre[0], k_pre[0], values[0], grad_out[0], segment_ids, gain_q, gain_k)
    out_q, out_k, sum_q, sum_k = pl.pallas_call(
        hand_out,
        out_shape=[
            jax.ShapeDtypeStruct(wide, BF16),
            jax.ShapeDtypeStruct(wide, BF16),
            jax.ShapeDtypeStruct(part, F32),
            jax.ShapeDtypeStruct(part, F32),
        ],
        in_specs=[pl.BlockSpec(memory_space=vmem)] * 2,
        out_specs=[anywhere] * 4,
        scratch_shapes=[dma((4,))],
    )(result, sums)
    return out_q[None], out_k[None], sum_q, sum_k


def solution(mesh):
    tokens = P("dp", "fsdp", None)
    return jax.shard_map(
        per_device,
        mesh=mesh,
        in_specs=(tokens, tokens, tokens, tokens, P("dp", "fsdp"), P(), P()),
        out_specs=(tokens, tokens, P(), P()),
        check_vma=False,
    )
```

```python
import math

import jax
import jax.numpy as jnp
from jax import lax
from jax.experimental import pallas as pl
from jax.experimental.pallas import tpu as pltpu
from jax.sharding import PartitionSpec as P

MESH = pl.DeviceIdType.MESH
F32 = jnp.float32
BF16 = jnp.bfloat16

HEADS = 24
DEPTH = 128
ROWS = 128
HALF = ROWS // 2
WIDTH = HEADS * DEPTH
PER_STEP = 2
STEPS = HEADS // PER_STEP
COLS = PER_STEP * DEPTH
SCALE = DEPTH**-0.5
SCALE_LOG2 = SCALE * math.log2(math.e)


def dot(a, b, contract_a, contract_b):
    dims = (((contract_a,), (contract_b,)), ((), ()))
    return lax.dot_general(a, b, dims, preferred_element_type=F32)


def lane_mean(x):
    return jnp.sum(x, -1, keepdims=True) * (1.0 / DEPTH)


def normalize(x, gain):
    centered = x - lane_mean(x)
    inverse = lax.rsqrt(lane_mean(centered * centered) + 1e-06)
    unit = centered * inverse
    return unit, inverse, (unit * gain).astype(BF16)


def normalize_back(grad, unit, inverse, gain):
    d_unit = grad * gain
    mean = lane_mean(d_unit)
    slope = lane_mean(d_unit * unit)
    return (inverse * (d_unit - mean - unit * slope)).astype(BF16)


def attention_back(queries, keys, values, cotangent, bias):
    scores = dot(keys, queries, 1, 1) * SCALE_LOG2 + bias
    expo = jnp.exp2(scores - jnp.max(scores, 0, keepdims=True))
    total = jnp.sum(expo, 0, keepdims=True)
    dprob = dot(values, cotangent, 1, 1)
    delta = jnp.sum(expo * dprob, 0, keepdims=True) / total
    slopes = (expo * (SCALE / total) * (dprob - delta)).astype(BF16)
    return dot(slopes, keys, 0, 0), dot(slopes, queries, 1, 0)


def place():
    f = lax.axis_index("fsdp")
    return lax.axis_index("dp"), f // 16, lax.rem(f, 16) // 2, lax.rem(f, 2)


def groups():
    y, x, z, c = place()
    return {
        "core": (2, c, lambda j: {"fsdp": x * 16 + z * 2 + j}),
        "x": (4, x, lambda j: {"fsdp": j * 16 + z * 2 + c}),
        "y": (8, y, lambda j: {"dp": j}),
        "z": (8, z, lambda j: {"fsdp": x * 16 + j * 2 + c}),
    }


def signal_around(sem, axes, distance):
    for name in axes:
        size, me, member = groups()[name]
        for step in (distance, size - distance):
            peer = member(lax.rem(me + step, size))
            pl.semaphore_signal(sem, inc=1, device_id=peer, device_id_type=MESH)
    return 2 * len(axes)


def kernel(
    q_ref, k_ref, v_ref, g_ref, ids_ref, gain_q_ref, gain_k_ref,
    result, sum_ref,
    own, halo, sent_back, came_back, gains, d_gains,
    ids_in, ids_own, ids_near, bias, weight, given,
    core_in, x_in, y_in, z_in,
    local_sem, id_send, id_recv, far_send, far_recv, back_send, back_recv,
    core_sem, x_sem, y_sem, z_sem, heard_1, heard_2,
):
    f = lax.axis_index("fsdp")
    size = lax.axis_size("fsdp")
    left = {"fsdp": lax.rem(f + size - 1, size)}
    right = {"fsdp": lax.rem(f + 1, size)}
    barrier = pltpu.get_barrier_semaphore()
    for device in (left, right):
        pl.semaphore_signal(barrier, inc=1, device_id=device, device_id_type=MESH)
    count = 2 + signal_around(barrier, "xyz", 1)

    sources = (q_ref, k_ref, v_ref, g_ref)
    loads = [pltpu.make_async_copy(ids_ref, ids_in, local_sem.at[4])]
    loads += [pltpu.make_async_copy(s, own.at[i], local_sem.at[i]) for i, s in enumerate(sources)]
    loads += [
        pltpu.make_async_copy(gain_q_ref, gains.at[0], local_sem.at[5]),
        pltpu.make_async_copy(gain_k_ref, gains.at[1], local_sem.at[6]),
    ]
    for load in loads:
        load.start()
    loads[0].wait()
    ids_own[...] = jnp.broadcast_to(ids_in[...], (8, ROWS))
    pl.semaphore_wait(barrier, count)

    def id_copy(side):
        return pltpu.make_async_remote_copy(
            src_ref=ids_own, dst_ref=ids_near.at[side], send_sem=id_send.at[side], recv_sem=id_recv.at[side],
            device_id=(left, right)[side], device_id_type=MESH,
        )

    def far_copy(step, array, side):
        rows = pl.ds(side * HALF, HALF)
        columns = pl.ds(pl.multiple_of(step * COLS, COLS), COLS)
        return pltpu.make_async_remote_copy(
            src_ref=sources[array].at[rows, columns], dst_ref=halo.at[array, rows, columns],
            send_sem=far_send.at[side, array, step], recv_sem=far_recv.at[side, array, step],
            device_id=(left, right)[side], device_id_type=MESH,
        )

    def back_copy(step, array, side):
        rows = pl.ds(side * HALF, HALF)
        columns = pl.ds(pl.multiple_of(step * COLS, COLS), COLS)
        return pltpu.make_async_remote_copy(
            src_ref=sent_back.at[array, rows, columns], dst_ref=came_back.at[array, rows, columns],
            send_sem=back_send.at[side, array, step], recv_sem=back_recv.at[side, array, step],
            device_id=(right, left)[side], device_id_type=MESH,
        )

    for side in (0, 1):
        id_copy(side).start()

    def send_far(step, carry):
        for array in range(4):
            for side in (0, 1):
                far_copy(step, array, side).start()
        return carry

    lax.fori_loop(0, STEPS, send_far, 0)
    near = signal_around(heard_1, "xyz", 1)

    for side in (0, 1):
        id_copy(side).wait()
    mine = ids_own[0:1, :]
    after = jnp.where(f < size - 1, ids_near[0, 0:1, :], -2)
    before = jnp.where(f > 0, ids_near[1, 0:1, :], -2)
    lane = lax.broadcasted_iota(jnp.int32, (1, ROWS), 1)

    def pick(x, at):
        return jnp.sum(jnp.where(lane == at, x, 0), -1, keepdims=True)

    first, last = pick(mine, 0), pick(mine, ROWS - 1)
    tail_before, head_after = pick(before, ROWS - 1), pick(after, 0)
    half_before, half_mine = pick(before, HALF - 1), pick(mine, HALF - 1)
    in_left = mine == tail_before
    in_right = mine == head_after
    take_left = half_before != first
    take_right = half_mine == last
    low = lane < HALF
    use_right = low & (after == last) & take_right
    use_left = (~low) & (before == first) & take_left
    halo_ids = jnp.where(use_right | use_left, jnp.where(low, after, before), -1)
    given_row = ((in_left & ~take_left) | (in_right & ~take_right)).astype(F32)
    used_row = (use_right | use_left).astype(F32)
    ids_row = jnp.concatenate([mine, halo_ids], 1).astype(F32)
    across = jnp.broadcast_to(ids_row, (2 * ROWS, 2 * ROWS))
    bias[...] = jnp.where(across == across.T, 0.0, -1e30).astype(F32)
    weight_row = jnp.concatenate([1.0 - given_row, used_row], 1)
    weight[...] = jnp.broadcast_to(weight_row, (ROWS, 2 * ROWS)).T
    given[...] = jnp.broadcast_to(given_row, (ROWS, ROWS)).T

    pl.semaphore_wait(heard_1, near)
    next_near = signal_around(heard_2, "yz", 2)
    for load in loads[1:]:
        load.wait()

    def compute(step, carry):
        for array in range(4):
            for side in (0, 1):
                far_copy(step, array, side).wait_recv()
        for part in range(PER_STEP):
            head = step * PER_STEP + part
            columns = pl.ds(pl.multiple_of(head * DEPTH, DEPTH), DEPTH)
            gain = [gains[i, pl.ds(head, 1), :] for i in range(2)]
            raw = [jnp.concatenate([own[i, :, columns], halo[i, :, columns]], 0) for i in range(4)]
            unit, inverse, normed = zip(*[normalize(raw[i].astype(F32), gain[i]) for i in range(2)])
            grads = attention_back(normed[0], normed[1], raw[2], raw[3], bias[...])
            for i in range(2):
                d_gains[i, pl.ds(head, 1), :] = jnp.sum(grads[i] * unit[i] * weight[...], 0, keepdims=True)
                d_raw = normalize_back(grads[i], unit[i], inverse[i], gain[i])
                result[i, :, columns] = d_raw[:ROWS]
                sent_back[i, :, columns] = d_raw[ROWS:]
        for array in range(2):
            for side in (0, 1):
                back_copy(step, array, side).start()
        return carry

    lax.fori_loop(0, STEPS, compute, 0)

    pl.semaphore_wait(heard_2, next_near)
    members = groups()
    core = members["core"][1]
    swap = pltpu.make_async_remote_copy(
        src_ref=d_gains, dst_ref=core_in, send_sem=core_sem.at[0], recv_sem=core_sem.at[1],
        device_id=members["core"][2](1 - core), device_id_type=MESH,
    )
    swap.start()
    swap.wait()

    def exchange(name, block, slots, sems):
        size, me, member = members[name]
        slots[me] = block.astype(BF16)
        copies = []
        for i in range(1, size):
            peer = lax.rem(me + i, size)
            copies.append(
                pltpu.make_async_remote_copy(
                    src_ref=slots.at[me], dst_ref=slots.at[me], send_sem=sems.at[0, i], recv_sem=sems.at[1, size - i],
                    device_id=member(peer), device_id_type=MESH,
                )
            )
        for copy in copies:
            copy.start()
        return copies

    def total(slots, copies):
        for copy in copies:
            copy.wait()
        return jnp.sum(slots[...].astype(F32), 0)

    copies = exchange("x", d_gains[...].reshape(2 * HEADS, DEPTH) + core_in[...].reshape(2 * HEADS, DEPTH), x_in, x_sem)
    copies = exchange("y", total(x_in, copies), y_in, y_sem)
    copies = exchange("z", total(y_in, copies), z_in, z_sem)

    def finish(step, carry):
        for array in range(2):
            for side in (0, 1):
                back_copy(step, array, side).wait_recv()
        for part in range(PER_STEP):
            columns = pl.ds(pl.multiple_of(step * COLS + part * DEPTH, DEPTH), DEPTH)
            away = given[...] != 0.0
            for i in range(2):
                mixed = jnp.where(away, came_back[i, :, columns].astype(F32), result[i, :, columns].astype(F32))
                result[i, :, columns] = mixed.astype(BF16)
        return carry

    lax.fori_loop(0, STEPS, finish, 0)
    sum_ref[...] = total(z_in, copies).reshape(2, HEADS, DEPTH)

    def drain(step, carry):
        for side in (0, 1):
            for array in range(4):
                far_copy(step, array, side).wait_send()
            for array in range(2):
                back_copy(step, array, side).wait_send()
        return carry

    lax.fori_loop(0, STEPS, drain, 0)


def hand_out(result, sums, out_q, out_k, sum_q, sum_k, sem):
    copies = [pltpu.make_async_copy(result.at[i], out, sem.at[i]) for i, out in enumerate((out_q, out_k))]
    copies += [pltpu.make_async_copy(sums.at[i], out, sem.at[2 + i]) for i, out in enumerate((sum_q, sum_k))]
    for copy in copies:
        copy.start()
    for copy in copies:
        copy.wait()


def per_device(q_pre, k_pre, values, grad_out, segment_ids, gain_q, gain_k):
    anywhere = pl.BlockSpec(memory_space=pl.ANY)
    vmem, dma = pltpu.VMEM, pltpu.SemaphoreType.DMA
    wide = (ROWS, WIDTH)
    part = (HEADS, DEPTH)
    result, sums = pl.pallas_call(
        kernel,
        out_shape=[vmem((2,) + wide, BF16), vmem((2,) + part, F32)],
        in_specs=[anywhere] * 7,
        out_specs=[pl.BlockSpec(memory_space=vmem)] * 2,
        scratch_shapes=[
            vmem((4,) + wide, BF16),
            vmem((4,) + wide, BF16),
            vmem((2,) + wide, BF16),
            vmem((2,) + wide, BF16),
            vmem((2,) + part, F32),
            vmem((2,) + part, F32),
            vmem((1, ROWS), jnp.int32),
            vmem((8, ROWS), jnp.int32),
            vmem((2, 8, ROWS), jnp.int32),
            vmem((2 * ROWS, 2 * ROWS), F32),
            vmem((2 * ROWS, ROWS), F32),
            vmem((ROWS, ROWS), F32),
            vmem((2,) + part, F32),
            vmem((4, 2 * HEADS, DEPTH), BF16),
            vmem((8, 2 * HEADS, DEPTH), BF16),
            vmem((8, 2 * HEADS, DEPTH), BF16),
            dma((7,)),
            dma((2,)),
            dma((2,)),
            dma((2, 4, STEPS)),
            dma((2, 4, STEPS)),
            dma((2, 2, STEPS)),
            dma((2, 2, STEPS)),
            dma((2,)),
            dma((2, 4)),
            dma((2, 8)),
            dma((2, 8)),
            pltpu.SemaphoreType.REGULAR,
            pltpu.SemaphoreType.REGULAR,
        ],
        compiler_params=pltpu.CompilerParams(
            collective_id=0, has_side_effects=True, vmem_limit_bytes=56 * 1024 * 1024
        ),
        cost_estimate=pl.CostEstimate(
            flops=HEADS * 8 * 256 * 256 * 128, bytes_accessed=5 << 20, transcendentals=HEADS * 256 * 256
        ),
    )(q_pre[0], k_pre[0], values[0], grad_out[0], segment_ids, gain_q, gain_k)
    out_q, out_k, sum_q, sum_k = pl.pallas_call(
        hand_out,
        out_shape=[
            jax.ShapeDtypeStruct(wide, BF16),
            jax.ShapeDtypeStruct(wide, BF16),
            jax.ShapeDtypeStruct(part, F32),
            jax.ShapeDtypeStruct(part, F32),
        ],
        in_specs=[pl.BlockSpec(memory_space=vmem)] * 2,
        out_specs=[anywhere] * 4,
        scratch_shapes=[dma((4,))],
        compiler_params=pltpu.CompilerParams(vmem_limit_bytes=4 * 1024 * 1024),
    )(result, sums)
    return out_q[None], out_k[None], sum_q, sum_k


def solution(mesh):
    tokens = P("dp", "fsdp", None)
    return jax.shard_map(
        per_device,
        mesh=mesh,
        in_specs=(tokens, tokens, tokens, tokens, P("dp", "fsdp"), P(), P()),
        out_specs=(tokens, tokens, P(), P()),
        check_vma=False,
    )
```

```python
import math

import jax
import jax.numpy as jnp
from jax import lax
from jax.experimental import pallas as pl
from jax.experimental.pallas import tpu as pltpu
from jax.sharding import PartitionSpec as P

MESH = pl.DeviceIdType.MESH
F32 = jnp.float32
BF16 = jnp.bfloat16

HEADS = 24
DEPTH = 128
ROWS = 128
WIDTH = HEADS * DEPTH
NEAR_HEADS = HEADS // 2
NEAR_WIDTH = NEAR_HEADS * DEPTH
AT_ONCE = 4
TILE = 16
TILES = ROWS // TILE
SLOTS = 56
PIECES = (0, 32, 40, 48, 56)
MOST = (20, 19, 16, 13, 11, 8, 5, 4)
PLACES = ((0, 1, 2, 3), (16, 17, 18, 19), (4, 5, 6, 7), (8, 9, 10, 11), (12, 13, 14, 15))
SCALE = DEPTH**-0.5
SCALE_LOG2 = SCALE * math.log2(math.e)


def dot(a, b, contract_a, contract_b):
    dims = (((contract_a,), (contract_b,)), ((), ()))
    return lax.dot_general(a, b, dims, preferred_element_type=F32)


def lane_mean(x):
    return jnp.sum(x, -1, keepdims=True) * (1.0 / DEPTH)


def normalize(x, gain):
    centered = x - lane_mean(x)
    inverse = lax.rsqrt(lane_mean(centered * centered) + 1e-06)
    unit = centered * inverse
    return unit, inverse, (unit * gain).astype(BF16)


def normalize_back(grad, unit, inverse, gain):
    d_unit = grad * gain
    mean = lane_mean(d_unit)
    slope = lane_mean(d_unit * unit)
    return (inverse * (d_unit - mean - unit * slope)).astype(BF16)


def diagonal(pair):
    zero = jnp.zeros((DEPTH, DEPTH), BF16)
    return jnp.concatenate(
        [jnp.concatenate([pair[0], zero], 1), jnp.concatenate([zero, pair[1]], 1)], 0
    )


def attention_back(queries, keys, values, cotangent, bias):
    both_keys = jnp.concatenate(keys, 1)
    both_queries = diagonal(queries)
    scores = dot(both_keys, both_queries, 1, 1) * SCALE_LOG2 + jnp.concatenate([bias, bias], 1)
    expo = jnp.exp2(scores - jnp.max(scores, 0, keepdims=True))
    total = jnp.sum(expo, 0, keepdims=True)
    dprob = dot(jnp.concatenate(values, 1), diagonal(cotangent), 1, 1)
    delta = jnp.sum(expo * dprob, 0, keepdims=True) / total
    slopes = (expo * (SCALE / total) * (dprob - delta)).astype(BF16)
    dq = dot(slopes, both_keys, 0, 0)
    dk = dot(slopes, both_queries, 1, 0)
    return [dq[:ROWS, :DEPTH], dq[ROWS:, DEPTH:]], [dk[:, :DEPTH], dk[:, DEPTH:]]


def place():
    f = lax.axis_index("fsdp")
    return lax.axis_index("dp"), f // 16, lax.rem(f, 16) // 2, lax.rem(f, 2)


def groups():
    y, x, z, c = place()
    return {
        "core": (2, c, lambda j: {"fsdp": x * 16 + z * 2 + j}),
        "x": (4, x, lambda j: {"fsdp": j * 16 + z * 2 + c}),
        "y": (8, y, lambda j: {"dp": j}),
        "z": (8, z, lambda j: {"fsdp": x * 16 + j * 2 + c}),
    }


def signal_around(sem, axes, distance):
    for name in axes:
        size, me, member = groups()[name]
        for step in (distance, size - distance):
            peer = member(lax.rem(me + step, size))
            pl.semaphore_signal(sem, inc=1, device_id=peer, device_id_type=MESH)
    return 2 * len(axes)


def kernel(
    q_ref, k_ref, v_ref, g_ref, ids_ref, gain_q_ref, gain_k_ref,
    result, sum_ref,
    own, near_in, near_out, near_back, packed, arrived,
    far_out, back_packed, back_tiles, gains, d_gains,
    ids_in, ids_own, ids_next, bias, weight, masks, own_terms, counts, cases, window,
    core_in, x_in, y_in, z_in,
    local_sem, near_id_sem, far_id_sem, near_sem, far_sem, near_back_sem, far_back_sem,
    core_sem, x_sem, y_sem, z_sem, heard_1, heard_2,
):
    f = lax.axis_index("fsdp")
    size = lax.axis_size("fsdp")
    core = lax.rem(f, 2)
    left, right = lax.rem(f + size - 1, size), lax.rem(f + 1, size)
    near = {"fsdp": f + 1 - 2 * core}
    far = {"fsdp": lax.rem(f + size - 1 + 2 * core, size)}
    barrier = pltpu.get_barrier_semaphore()
    for device in (left, right):
        pl.semaphore_signal(barrier, inc=1, device_id={"fsdp": device}, device_id_type=MESH)
    count = 2 + signal_around(barrier, "xyz", 1)

    sources = (q_ref, k_ref, v_ref, g_ref)
    loads = [pltpu.make_async_copy(ids_ref, ids_in, local_sem.at[4])]
    loads += [pltpu.make_async_copy(s, own.at[i], local_sem.at[i]) for i, s in enumerate(sources)]
    loads += [
        pltpu.make_async_copy(gain_q_ref, gains.at[0], local_sem.at[5]),
        pltpu.make_async_copy(gain_k_ref, gains.at[1], local_sem.at[6]),
    ]
    for load in loads:
        load.start()
    loads[0].wait()
    ids_own[...] = jnp.broadcast_to(ids_in[...], (8, ROWS))

    def remote(source, target, pair, device):
        return pltpu.make_async_remote_copy(
            src_ref=source, dst_ref=target, send_sem=pair.at[0], recv_sem=pair.at[1],
            device_id=device, device_id_type=MESH,
        )

    mine = ids_own[0:1, :]
    lane = lax.broadcasted_iota(jnp.int32, (1, ROWS), 1)

    def down(row):
        return jnp.broadcast_to(row, (ROWS, ROWS)).T

    def set_bias(place, row):
        across = jnp.broadcast_to(row, (ROWS, ROWS))
        bias[place] = jnp.where(across == across.T, 0.0, -1e30).astype(F32)

    def head_columns(head):
        return pl.ds(pl.multiple_of(head * DEPTH, DEPTH), DEPTH)

    def image_back(raw, heads, place):
        gain = [[gains[i, pl.ds(head, 1), :] for head in heads] for i in range(2)]
        normed = [[normalize(raw[i][h].astype(F32), gain[i][h]) for h in range(2)] for i in range(2)]
        halves = [[normed[i][h][2] for h in range(2)] for i in range(2)]
        grads = attention_back(halves[0], halves[1], raw[2], raw[3], bias[place])
        terms = [[grads[i][h] * normed[i][h][0] for h in range(2)] for i in range(2)]
        d_raw = [
            [normalize_back(grads[i][h], normed[i][h][0], normed[i][h][1], gain[i][h]) for h in range(2)]
            for i in range(2)
        ]
        return d_raw, terms

    def weigh(term, place):
        return jnp.sum(term * weight[place], 0, keepdims=True)

    def alone(step, carry):
        for part in range(AT_ONCE // 2):
            heads = [step * AT_ONCE + part * 2 + h for h in range(2)]
            columns = [head_columns(head) for head in heads]
            d_raw, terms = image_back([[own[i, :, c] for c in columns] for i in range(4)], heads, 0)
            for i in range(2):
                for h in range(2):
                    result[i, :, columns[h]] = d_raw[i][h]
                    own_terms[heads[h], i] = terms[i][h]
        return carry

    def sum_alone(head, carry):
        for i in range(2):
            d_gains[i, pl.ds(head, 1), :] = weigh(own_terms[head, i], 0)
        return carry

    set_bias(0, mine.astype(F32))
    for load in loads[1:]:
        load.wait()
    lax.fori_loop(0, 2, alone, 0)
    pl.semaphore_wait(barrier, count)

    id_copies = [
        remote(ids_own, ids_next.at[i], sems, device)
        for i, sems, device in ((0, near_id_sem, near), (1, far_id_sem, far))
    ]
    for copy in id_copies:
        copy.start()
    away = pl.ds(pl.multiple_of((1 - core) * NEAR_WIDTH, DEPTH), NEAR_WIDTH)
    near_copies = [remote(own.at[i, :, away], near_in.at[i], near_sem.at[i], near) for i in range(4)]
    for copy in near_copies:
        copy.start()
    heard = signal_around(heard_1, "xyz", 1)

    lax.fori_loop(2, 4, alone, 0)
    for copy in id_copies:
        copy.wait()
    pl.semaphore_wait(heard_1, heard)
    next_heard = signal_around(heard_2, "yz", 2)

    def pick(x, at):
        return jnp.sum(jnp.where(lane == at, x, 0), -1, keepdims=True)

    def shared(other, at_end):
        my_edge = jnp.where(at_end, ROWS - 1, 0)
        own_rows = mine == pick(other, ROWS - 1 - my_edge)
        other_rows = other == pick(mine, my_edge)
        return own_rows, other_rows

    follows = core == 1
    has_far = jnp.where(follows, f < size - 1, f > 0)
    far_ids = jnp.where(has_far, ids_next[1, 0:1, :], -2)
    near_own, near_other = shared(ids_next[0, 0:1, :], core == 0)
    far_own, far_other = shared(far_ids, follows)
    near_used, far_used = near_own | near_other, far_own | far_other
    set_bias(1, near_used.astype(F32))
    set_bias(2, far_used.astype(F32))
    weight[0] = down(1.0 - (near_own | far_own).astype(F32))
    weight[1] = down(near_used.astype(F32))
    weight[2] = down(far_used.astype(F32))
    for i, row in enumerate((near_own, near_other, far_own, far_other)):
        masks[i] = down(row.astype(F32)).astype(BF16)

    def tiles_of(rows):
        return (jnp.sum(rows.astype(jnp.int32), -1, keepdims=True) + (TILE - 1)) >> 4

    my_tiles, other_tiles = tiles_of(far_own), tiles_of(far_other)
    begin_tiles = jnp.where(follows, my_tiles, other_tiles)
    split = jnp.full((1, 1), 4, jnp.int32)
    for least, more in ((2, 1), (3, 3), (4, 3), (5, 2), (6, 3), (7, 3), (8, 1)):
        split = split + jnp.where(begin_tiles >= least, more, 0)
    rest = HEADS - split
    counts[0:1, :] = jnp.broadcast_to(jnp.where(follows, split, rest), (1, DEPTH))
    counts[1:2, :] = jnp.broadcast_to(jnp.where(follows, rest, split), (1, DEPTH))
    for case in range(TILES):
        for i, tiles in enumerate((my_tiles, other_tiles)):
            cases[i, case] = jnp.broadcast_to((tiles == case + 1).astype(F32), (TILE, DEPTH)).astype(BF16)

    kept_heads = [core * p + (1 - core) * (HEADS - 1 - p) for p in range(MOST[0])]
    sent_heads = [core * (HEADS - 1 - p) + (1 - core) * p for p in range(MOST[0])]
    my_rows = [(core * (TILES - 1 - u) + (1 - core) * u) * TILE for u in range(TILES)]
    other_rows_at = [(core * u + (1 - core) * (TILES - 1 - u)) * TILE for u in range(TILES)]

    def tile_rows(starts, u):
        return pl.ds(pl.multiple_of(starts[u], TILE), TILE)

    def chosen(side, terms):
        block = None
        for case, value in terms:
            term = value * cases[side, case]
            block = term if block is None else block + term
        return jnp.zeros((TILE, DEPTH), BF16) if block is None else block

    def cases_of_slot(slot):
        return [(n - 1, slot // n, slot % n) for n in range(1, TILES + 1) if slot < MOST[n - 1] * n]

    def cases_of_tile(place, u):
        return [(n - 1, place * n + u) for n in range(u + 1, TILES + 1) if place < MOST[n - 1]]

    far_copies = []
    for piece in range(len(PIECES) - 1):
        for slot in range(PIECES[piece], PIECES[piece + 1]):
            for i in range(4):
                packed[slot, i] = chosen(
                    0,
                    [
                        (case, own[i, tile_rows(my_rows, u), head_columns(sent_heads[place])])
                        for case, place, u in cases_of_slot(slot)
                    ],
                )
        span = pl.ds(PIECES[piece], PIECES[piece + 1] - PIECES[piece])
        copy = remote(packed.at[span], arrived.at[span], far_sem.at[piece], far)
        copy.start()
        far_copies.append(copy)

    lax.fori_loop(4, HEADS // AT_ONCE, alone, 0)
    lax.fori_loop(0, HEADS, sum_alone, 0, unroll=2)

    def between_cores(step, carry):
        own_rows, other_rows = masks[0] != 0, masks[1] != 0
        for part in range(AT_ONCE // 2):
            places = [step * AT_ONCE + part * 2 + h for h in range(2)]
            heads = [core * NEAR_HEADS + place for place in places]
            columns, inner = [head_columns(h) for h in heads], [head_columns(p) for p in places]
            raw = [
                [jnp.where(other_rows, near_in[i, :, inner[h]], own[i, :, columns[h]]) for h in range(2)]
                for i in range(4)
            ]
            d_raw, terms = image_back(raw, heads, 1)
            for i in range(2):
                for h in range(2):
                    result[i, :, columns[h]] = jnp.where(own_rows, d_raw[i][h], result[i, :, columns[h]])
                    near_out[i, :, inner[h]] = d_raw[i][h]
                    d_gains[i, pl.ds(heads[h], 1), :] += weigh(terms[i][h], 1)
        return carry

    for copy in near_copies:
        copy.wait_recv()
    lax.fori_loop(0, NEAR_HEADS // AT_ONCE, between_cores, 0)
    near_return = remote(near_out, near_back, near_back_sem, near)
    near_return.start()

    def between_chips(places):
        other_rows = masks[3] != 0
        for h, place in enumerate(places):
            for u in range(TILES):
                for i in range(4):
                    window[h, i, tile_rows(other_rows_at, u), :] = chosen(
                        1, [(case, arrived[slot, i]) for case, slot in cases_of_tile(place, u)]
                    )
        for first in range(0, len(places), 2):
            pair = places[first : first + 2]
            heads = [kept_heads[place] for place in pair]
            columns = [head_columns(head) for head in heads]
            here = [(counts[0:1, :] > place).astype(F32) for place in pair]
            raw = [
                [jnp.where(other_rows, window[first + h, i], own[i, :, columns[h]]) for h in range(2)]
                for i in range(4)
            ]
            d_raw, terms = image_back(raw, heads, 2)
            for h in range(2):
                changed = masks[2] * here[h].astype(BF16) != 0
                for i in range(2):
                    result[i, :, columns[h]] = jnp.where(changed, d_raw[i][h], result[i, :, columns[h]])
                    far_out[pair[h], i] = d_raw[i][h]
                    d_gains[i, pl.ds(heads[h], 1), :] += weigh(terms[i][h], 2) * here[h]

    waited = 0
    for places in PLACES:
        need = 1 + max(slot for p in places for u in range(TILES) for _, slot in cases_of_tile(p, u))
        while PIECES[waited] < need:
            far_copies[waited].wait_recv()
            waited += 1
        between_chips(places)

    pl.semaphore_wait(heard_2, next_heard)
    swap = remote(d_gains, core_in, core_sem, near)
    swap.start()

    members = groups()

    def exchange(name, block, slots, sems):
        size, me, member = members[name]
        slots[me] = block.astype(BF16)
        copies = []
        for i in range(1, size):
            peer = lax.rem(me + i, size)
            copies.append(
                pltpu.make_async_remote_copy(
                    src_ref=slots.at[me], dst_ref=slots.at[me], send_sem=sems.at[0, i], recv_sem=sems.at[1, size - i],
                    device_id=member(peer), device_id_type=MESH,
                )
            )
        for copy in copies:
            copy.start()
        return copies

    def total(slots, copies):
        for copy in copies:
            copy.wait()
        return jnp.sum(slots[...].astype(F32), 0)

    swap.wait()
    chip = d_gains[...].reshape(2 * HEADS, DEPTH) + core_in[...].reshape(2 * HEADS, DEPTH)
    copies = exchange("x", chip, x_in, x_sem)
    for slot in range(SLOTS):
        for i in range(2):
            back_packed[slot, i] = chosen(
                1,
                [
                    (case, far_out[place, i, tile_rows(other_rows_at, u), :])
                    for case, place, u in cases_of_slot(slot)
                ],
            )
    far_return = remote(back_packed, back_tiles, far_back_sem, far)
    far_return.start()
    copies = exchange("y", total(x_in, copies), y_in, y_sem)

    near_return.wait()

    def finish_near(place, carry):
        columns, inner = head_columns((1 - core) * NEAR_HEADS + place), head_columns(place)
        for i in range(2):
            result[i, :, columns] = jnp.where(masks[0] != 0, near_back[i, :, inner], result[i, :, columns])
        return carry

    lax.fori_loop(0, NEAR_HEADS, finish_near, 0)
    copies = exchange("z", total(y_in, copies), z_in, z_sem)
    far_return.wait()

    for place in range(MOST[0]):
        columns = head_columns(sent_heads[place])
        theirs = masks[2] * (counts[1:2, :] > place).astype(F32).astype(BF16) != 0
        for i in range(2):
            for u in range(TILES):
                window[place % 4, i, tile_rows(my_rows, u), :] = chosen(
                    0, [(case, back_tiles[slot, i]) for case, slot in cases_of_tile(place, u)]
                )
            result[i, :, columns] = jnp.where(theirs, window[place % 4, i], result[i, :, columns])
    sum_ref[...] = total(z_in, copies).reshape(2, HEADS, DEPTH)
    for copy in near_copies + far_copies:
        copy.wait_send()


def hand_out(result, sums, out_q, out_k, sum_q, sum_k, sem):
    copies = [pltpu.make_async_copy(result.at[i], out, sem.at[i]) for i, out in enumerate((out_q, out_k))]
    copies += [pltpu.make_async_copy(sums.at[i], out, sem.at[2 + i]) for i, out in enumerate((sum_q, sum_k))]
    for copy in copies:
        copy.start()
    for copy in copies:
        copy.wait()


def per_device(q_pre, k_pre, values, grad_out, segment_ids, gain_q, gain_k):
    anywhere = pl.BlockSpec(memory_space=pl.ANY)
    vmem, dma = pltpu.VMEM, pltpu.SemaphoreType.DMA
    wide = (ROWS, WIDTH)
    part = (HEADS, DEPTH)
    result, sums = pl.pallas_call(
        kernel,
        out_shape=[vmem((2,) + wide, BF16), vmem((2,) + part, F32)],
        in_specs=[anywhere] * 7,
        out_specs=[pl.BlockSpec(memory_space=vmem)] * 2,
        scratch_shapes=[
            vmem((4,) + wide, BF16),
            vmem((4, ROWS, NEAR_WIDTH), BF16),
            vmem((2, ROWS, NEAR_WIDTH), BF16),
            vmem((2, ROWS, NEAR_WIDTH), BF16),
            vmem((SLOTS, 4, TILE, DEPTH), BF16),
            vmem((SLOTS, 4, TILE, DEPTH), BF16),
            vmem((MOST[0], 2, ROWS, DEPTH), BF16),
            vmem((SLOTS, 2, TILE, DEPTH), BF16),
            vmem((SLOTS, 2, TILE, DEPTH), BF16),
            vmem((2,) + part, F32),
            vmem((2,) + part, F32),
            vmem((1, ROWS), jnp.int32),
            vmem((8, ROWS), jnp.int32),
            vmem((2, 8, ROWS), jnp.int32),
            vmem((3, ROWS, ROWS), F32),
            vmem((3, ROWS, ROWS), F32),
            vmem((4, ROWS, ROWS), BF16),
            vmem((HEADS, 2, ROWS, DEPTH), F32),
            vmem((8, DEPTH), jnp.int32),
            vmem((2, TILES, TILE, DEPTH), BF16),
            vmem((4, 4, ROWS, DEPTH), BF16),
            vmem((2,) + part, F32),
            vmem((4, 2 * HEADS, DEPTH), BF16),
            vmem((8, 2 * HEADS, DEPTH), BF16),
            vmem((8, 2 * HEADS, DEPTH), BF16),
            dma((7,)),
            dma((2,)),
            dma((2,)),
            dma((4, 2)),
            dma((len(PIECES) - 1, 2)),
            dma((2,)),
            dma((2,)),
            dma((2,)),
            dma((2, 4)),
            dma((2, 8)),
            dma((2, 8)),
            pltpu.SemaphoreType.REGULAR,
            pltpu.SemaphoreType.REGULAR,
        ],
        compiler_params=pltpu.CompilerParams(
            collective_id=0, has_side_effects=True, vmem_limit_bytes=56 * 1024 * 1024
        ),
        cost_estimate=pl.CostEstimate(
            flops=HEADS * 8 * 256 * 256 * 128, bytes_accessed=5 << 20, transcendentals=HEADS * 256 * 256
        ),
    )(q_pre[0], k_pre[0], values[0], grad_out[0], segment_ids, gain_q, gain_k)
    out_q, out_k, sum_q, sum_k = pl.pallas_call(
        hand_out,
        out_shape=[
            jax.ShapeDtypeStruct(wide, BF16),
            jax.ShapeDtypeStruct(wide, BF16),
            jax.ShapeDtypeStruct(part, F32),
            jax.ShapeDtypeStruct(part, F32),
        ],
        in_specs=[pl.BlockSpec(memory_space=vmem)] * 2,
        out_specs=[anywhere] * 4,
        scratch_shapes=[dma((4,))],
        compiler_params=pltpu.CompilerParams(vmem_limit_bytes=4 * 1024 * 1024),
    )(result, sums)
    return out_q[None], out_k[None], sum_q, sum_k


def solution(mesh):
    tokens = P("dp", "fsdp", None)
    return jax.shard_map(
        per_device,
        mesh=mesh,
        in_specs=(tokens, tokens, tokens, tokens, P("dp", "fsdp"), P(), P()),
        out_specs=(tokens, tokens, P(), P()),
        check_vma=False,
    )
```

```python
import math

import jax
import jax.numpy as jnp
from jax import lax
from jax.experimental import pallas as pl
from jax.experimental.pallas import tpu as pltpu
from jax.sharding import PartitionSpec as P

MESH = pl.DeviceIdType.MESH
F32 = jnp.float32
BF16 = jnp.bfloat16

HEADS = 24
DEPTH = 128
ROWS = 128
WIDTH = HEADS * DEPTH
NEAR_HEADS = HEADS // 2
NEAR_WIDTH = NEAR_HEADS * DEPTH
ALONE_AT_ONCE = 8
NEAR_AT_ONCE = 6
TILE = 16
TILES = ROWS // TILE
SLOTS = 56
PIECES = (0, 32, 40, 48, 56)
MOST = (20, 19, 16, 13, 11, 8, 5, 4)
PLACES = ((0, 1, 2, 3), (16, 17, 18, 19), (4, 5, 6, 7), (8, 9, 10, 11), (12, 13, 14, 15))
SCALE = DEPTH**-0.5
SCALE_LOG2 = SCALE * math.log2(math.e)


def dot(a, b, contract_a, contract_b):
    dims = (((contract_a,), (contract_b,)), ((), ()))
    return lax.dot_general(a, b, dims, preferred_element_type=F32)


def lane_mean(x):
    return jnp.sum(x, -1, keepdims=True) * (1.0 / DEPTH)


def normalize(x, gain):
    centered = x - lane_mean(x)
    inverse = lax.rsqrt(lane_mean(centered * centered) + 1e-06)
    unit = centered * inverse
    return unit, inverse, (unit * gain).astype(BF16)


def normalize_back(grad, unit, inverse, gain):
    d_unit = grad * gain
    mean = lane_mean(d_unit)
    slope = lane_mean(d_unit * unit)
    return (inverse * (d_unit - mean - unit * slope)).astype(BF16)


def diagonal(pair):
    zero = jnp.zeros((DEPTH, DEPTH), BF16)
    return jnp.concatenate(
        [jnp.concatenate([pair[0], zero], 1), jnp.concatenate([zero, pair[1]], 1)], 0
    )


def attention_back(queries, keys, values, cotangent, bias):
    both_keys = jnp.concatenate(keys, 1)
    both_queries = diagonal(queries)
    scores = dot(both_keys, both_queries, 1, 1) * SCALE_LOG2 + jnp.concatenate([bias, bias], 1)
    expo = jnp.exp2(scores - jnp.max(scores, 0, keepdims=True))
    total = jnp.sum(expo, 0, keepdims=True)
    dprob = dot(jnp.concatenate(values, 1), diagonal(cotangent), 1, 1)
    delta = jnp.sum(expo * dprob, 0, keepdims=True) / total
    slopes = (expo * (SCALE / total) * (dprob - delta)).astype(BF16)
    dq = dot(slopes, both_keys, 0, 0)
    dk = dot(slopes, both_queries, 1, 0)
    return [dq[:ROWS, :DEPTH], dq[ROWS:, DEPTH:]], [dk[:, :DEPTH], dk[:, DEPTH:]]


def place():
    f = lax.axis_index("fsdp")
    return lax.axis_index("dp"), f // 16, lax.rem(f, 16) // 2, lax.rem(f, 2)


def groups():
    y, x, z, c = place()
    return {
        "core": (2, c, lambda j: {"fsdp": x * 16 + z * 2 + j}),
        "x": (4, x, lambda j: {"fsdp": j * 16 + z * 2 + c}),
        "y": (8, y, lambda j: {"dp": j}),
        "z": (8, z, lambda j: {"fsdp": x * 16 + j * 2 + c}),
    }


def signal_around(sem, axes, distance):
    for name in axes:
        size, me, member = groups()[name]
        for step in (distance, size - distance):
            peer = member(lax.rem(me + step, size))
            pl.semaphore_signal(sem, inc=1, device_id=peer, device_id_type=MESH)
    return 2 * len(axes)


def kernel(
    q_ref, k_ref, v_ref, g_ref, ids_ref, gain_q_ref, gain_k_ref,
    result, sum_ref,
    own, near_in, near_out, near_back, packed, arrived,
    far_out, back_packed, back_tiles, gains, d_gains,
    ids_in, ids_own, ids_next, bias, weight, masks, own_terms, counts, cases, window,
    core_in, x_in, y_in, z_in,
    local_sem, near_id_sem, far_id_sem, near_sem, far_sem, near_back_sem, far_back_sem,
    core_sem, x_sem, y_sem, z_sem, heard_1, heard_2,
):
    f = lax.axis_index("fsdp")
    size = lax.axis_size("fsdp")
    core = lax.rem(f, 2)
    left, right = lax.rem(f + size - 1, size), lax.rem(f + 1, size)
    near = {"fsdp": f + 1 - 2 * core}
    far = {"fsdp": lax.rem(f + size - 1 + 2 * core, size)}
    barrier = pltpu.get_barrier_semaphore()
    for device in (left, right):
        pl.semaphore_signal(barrier, inc=1, device_id={"fsdp": device}, device_id_type=MESH)
    count = 2 + signal_around(barrier, "xyz", 1)

    sources = (q_ref, k_ref, v_ref, g_ref)
    loads = [pltpu.make_async_copy(ids_ref, ids_in, local_sem.at[4])]
    loads += [pltpu.make_async_copy(s, own.at[i], local_sem.at[i]) for i, s in enumerate(sources)]
    loads += [
        pltpu.make_async_copy(gain_q_ref, gains.at[0], local_sem.at[5]),
        pltpu.make_async_copy(gain_k_ref, gains.at[1], local_sem.at[6]),
    ]
    for load in loads:
        load.start()
    loads[0].wait()
    ids_own[...] = jnp.broadcast_to(ids_in[...], (8, ROWS))

    def remote(source, target, pair, device):
        return pltpu.make_async_remote_copy(
            src_ref=source, dst_ref=target, send_sem=pair.at[0], recv_sem=pair.at[1],
            device_id=device, device_id_type=MESH,
        )

    mine = ids_own[0:1, :]
    lane = lax.broadcasted_iota(jnp.int32, (1, ROWS), 1)

    def down(row):
        return jnp.broadcast_to(row, (ROWS, ROWS)).T

    def set_bias(place, row):
        across = jnp.broadcast_to(row, (ROWS, ROWS))
        bias[place] = jnp.where(across == across.T, 0.0, -1e30).astype(F32)

    def head_columns(head):
        return pl.ds(pl.multiple_of(head * DEPTH, DEPTH), DEPTH)

    def image_back(raw, heads, place):
        gain = [[gains[i, pl.ds(head, 1), :] for head in heads] for i in range(2)]
        normed = [[normalize(raw[i][h].astype(F32), gain[i][h]) for h in range(2)] for i in range(2)]
        halves = [[normed[i][h][2] for h in range(2)] for i in range(2)]
        grads = attention_back(halves[0], halves[1], raw[2], raw[3], bias[place])
        terms = [[grads[i][h] * normed[i][h][0] for h in range(2)] for i in range(2)]
        d_raw = [
            [normalize_back(grads[i][h], normed[i][h][0], normed[i][h][1], gain[i][h]) for h in range(2)]
            for i in range(2)
        ]
        return d_raw, terms

    def weigh(term, place):
        return jnp.sum(term * weight[place], 0, keepdims=True)

    def alone(step, carry):
        for part in range(ALONE_AT_ONCE // 2):
            heads = [step * ALONE_AT_ONCE + part * 2 + h for h in range(2)]
            columns = [head_columns(head) for head in heads]
            d_raw, terms = image_back([[own[i, :, c] for c in columns] for i in range(4)], heads, 0)
            for i in range(2):
                for h in range(2):
                    result[i, :, columns[h]] = d_raw[i][h]
                    own_terms[heads[h], i] = terms[i][h]
        return carry

    def sum_alone(head, carry):
        for i in range(2):
            d_gains[i, pl.ds(head, 1), :] = weigh(own_terms[head, i], 0)
        return carry

    set_bias(0, mine.astype(F32))
    for load in loads[1:]:
        load.wait()
    lax.fori_loop(0, 1, alone, 0)
    pl.semaphore_wait(barrier, count)

    id_copies = [
        remote(ids_own, ids_next.at[i], sems, device)
        for i, sems, device in ((0, near_id_sem, near), (1, far_id_sem, far))
    ]
    for copy in id_copies:
        copy.start()
    away = pl.ds(pl.multiple_of((1 - core) * NEAR_WIDTH, DEPTH), NEAR_WIDTH)
    near_copies = [remote(own.at[i, :, away], near_in.at[i], near_sem.at[i], near) for i in range(4)]
    for copy in near_copies:
        copy.start()
    heard = signal_around(heard_1, "xyz", 1)

    lax.fori_loop(1, 2, alone, 0)
    for copy in id_copies:
        copy.wait()
    pl.semaphore_wait(heard_1, heard)
    next_heard = signal_around(heard_2, "yz", 2)

    def pick(x, at):
        return jnp.sum(jnp.where(lane == at, x, 0), -1, keepdims=True)

    def shared(other, at_end):
        my_edge = jnp.where(at_end, ROWS - 1, 0)
        own_rows = mine == pick(other, ROWS - 1 - my_edge)
        other_rows = other == pick(mine, my_edge)
        return own_rows, other_rows

    follows = core == 1
    has_far = jnp.where(follows, f < size - 1, f > 0)
    far_ids = jnp.where(has_far, ids_next[1, 0:1, :], -2)
    near_own, near_other = shared(ids_next[0, 0:1, :], core == 0)
    far_own, far_other = shared(far_ids, follows)
    near_used, far_used = near_own | near_other, far_own | far_other
    set_bias(1, near_used.astype(F32))
    set_bias(2, far_used.astype(F32))
    weight[0] = down(1.0 - (near_own | far_own).astype(F32))
    weight[1] = down(near_used.astype(F32))
    weight[2] = down(far_used.astype(F32))
    for i, row in enumerate((near_own, near_other, far_own, far_other)):
        masks[i] = down(row.astype(F32)).astype(BF16)

    def tiles_of(rows):
        return (jnp.sum(rows.astype(jnp.int32), -1, keepdims=True) + (TILE - 1)) >> 4

    my_tiles, other_tiles = tiles_of(far_own), tiles_of(far_other)
    begin_tiles = jnp.where(follows, my_tiles, other_tiles)
    split = jnp.full((1, 1), 4, jnp.int32)
    for least, more in ((2, 1), (3, 3), (4, 3), (5, 2), (6, 3), (7, 3), (8, 1)):
        split = split + jnp.where(begin_tiles >= least, more, 0)
    rest = HEADS - split
    counts[0:1, :] = jnp.broadcast_to(jnp.where(follows, split, rest), (1, DEPTH))
    counts[1:2, :] = jnp.broadcast_to(jnp.where(follows, rest, split), (1, DEPTH))
    for case in range(TILES):
        for i, tiles in enumerate((my_tiles, other_tiles)):
            cases[i, case] = jnp.broadcast_to((tiles == case + 1).astype(F32), (TILE, DEPTH)).astype(BF16)

    kept_heads = [core * p + (1 - core) * (HEADS - 1 - p) for p in range(MOST[0])]
    sent_heads = [core * (HEADS - 1 - p) + (1 - core) * p for p in range(MOST[0])]
    my_rows = [(core * (TILES - 1 - u) + (1 - core) * u) * TILE for u in range(TILES)]
    other_rows_at = [(core * u + (1 - core) * (TILES - 1 - u)) * TILE for u in range(TILES)]

    def tile_rows(starts, u):
        return pl.ds(pl.multiple_of(starts[u], TILE), TILE)

    def chosen(side, terms):
        block = None
        for case, value in terms:
            term = value * cases[side, case]
            block = term if block is None else block + term
        return jnp.zeros((TILE, DEPTH), BF16) if block is None else block

    def cases_of_slot(slot):
        return [(n - 1, slot // n, slot % n) for n in range(1, TILES + 1) if slot < MOST[n - 1] * n]

    def cases_of_tile(place, u):
        return [(n - 1, place * n + u) for n in range(u + 1, TILES + 1) if place < MOST[n - 1]]

    far_copies = []
    for piece in range(len(PIECES) - 1):
        for slot in range(PIECES[piece], PIECES[piece + 1]):
            for i in range(4):
                packed[slot, i] = chosen(
                    0,
                    [
                        (case, own[i, tile_rows(my_rows, u), head_columns(sent_heads[place])])
                        for case, place, u in cases_of_slot(slot)
                    ],
                )
        span = pl.ds(PIECES[piece], PIECES[piece + 1] - PIECES[piece])
        copy = remote(packed.at[span], arrived.at[span], far_sem.at[piece], far)
        copy.start()
        far_copies.append(copy)

    lax.fori_loop(2, HEADS // ALONE_AT_ONCE, alone, 0)
    lax.fori_loop(0, HEADS, sum_alone, 0, unroll=4)

    def between_cores(step, carry):
        own_rows, other_rows = masks[0] != 0, masks[1] != 0
        for part in range(NEAR_AT_ONCE // 2):
            places = [step * NEAR_AT_ONCE + part * 2 + h for h in range(2)]
            heads = [core * NEAR_HEADS + place for place in places]
            columns, inner = [head_columns(h) for h in heads], [head_columns(p) for p in places]
            raw = [
                [jnp.where(other_rows, near_in[i, :, inner[h]], own[i, :, columns[h]]) for h in range(2)]
                for i in range(4)
            ]
            d_raw, terms = image_back(raw, heads, 1)
            for i in range(2):
                for h in range(2):
                    result[i, :, columns[h]] = jnp.where(own_rows, d_raw[i][h], result[i, :, columns[h]])
                    near_out[i, :, inner[h]] = d_raw[i][h]
                    d_gains[i, pl.ds(heads[h], 1), :] += weigh(terms[i][h], 1)
        return carry

    for copy in near_copies:
        copy.wait_recv()
    lax.fori_loop(0, NEAR_HEADS // NEAR_AT_ONCE, between_cores, 0)
    near_return = remote(near_out, near_back, near_back_sem, near)
    near_return.start()

    def between_chips(places):
        other_rows = masks[3] != 0
        for h, place in enumerate(places):
            for u in range(TILES):
                for i in range(4):
                    window[h, i, tile_rows(other_rows_at, u), :] = chosen(
                        1, [(case, arrived[slot, i]) for case, slot in cases_of_tile(place, u)]
                    )
        for first in range(0, len(places), 2):
            pair = places[first : first + 2]
            heads = [kept_heads[place] for place in pair]
            columns = [head_columns(head) for head in heads]
            here = [(counts[0:1, :] > place).astype(F32) for place in pair]
            raw = [
                [jnp.where(other_rows, window[first + h, i], own[i, :, columns[h]]) for h in range(2)]
                for i in range(4)
            ]
            d_raw, terms = image_back(raw, heads, 2)
            for h in range(2):
                changed = masks[2] * here[h].astype(BF16) != 0
                for i in range(2):
                    result[i, :, columns[h]] = jnp.where(changed, d_raw[i][h], result[i, :, columns[h]])
                    far_out[pair[h], i] = d_raw[i][h]
                    d_gains[i, pl.ds(heads[h], 1), :] += weigh(terms[i][h], 2) * here[h]

    waited = 0
    for places in PLACES:
        need = 1 + max(slot for p in places for u in range(TILES) for _, slot in cases_of_tile(p, u))
        while PIECES[waited] < need:
            far_copies[waited].wait_recv()
            waited += 1
        between_chips(places)

    pl.semaphore_wait(heard_2, next_heard)
    swap = remote(d_gains, core_in, core_sem, near)
    swap.start()

    members = groups()

    def exchange(name, block, slots, sems):
        size, me, member = members[name]
        slots[me] = block.astype(BF16)
        copies = []
        for i in range(1, size):
            peer = lax.rem(me + i, size)
            copies.append(
                pltpu.make_async_remote_copy(
                    src_ref=slots.at[me], dst_ref=slots.at[me], send_sem=sems.at[0, i], recv_sem=sems.at[1, size - i],
                    device_id=member(peer), device_id_type=MESH,
                )
            )
        for copy in copies:
            copy.start()
        return copies

    def total(slots, copies):
        for copy in copies:
            copy.wait()
        return jnp.sum(slots[...].astype(F32), 0)

    swap.wait()
    chip = d_gains[...].reshape(2 * HEADS, DEPTH) + core_in[...].reshape(2 * HEADS, DEPTH)
    copies = exchange("x", chip, x_in, x_sem)
    for slot in range(SLOTS):
        for i in range(2):
            back_packed[slot, i] = chosen(
                1,
                [
                    (case, far_out[place, i, tile_rows(other_rows_at, u), :])
                    for case, place, u in cases_of_slot(slot)
                ],
            )
    far_return = remote(back_packed, back_tiles, far_back_sem, far)
    far_return.start()
    copies = exchange("y", total(x_in, copies), y_in, y_sem)

    near_return.wait()

    def finish_near(place, carry):
        columns, inner = head_columns((1 - core) * NEAR_HEADS + place), head_columns(place)
        for i in range(2):
            result[i, :, columns] = jnp.where(masks[0] != 0, near_back[i, :, inner], result[i, :, columns])
        return carry

    lax.fori_loop(0, NEAR_HEADS, finish_near, 0)
    copies = exchange("z", total(y_in, copies), z_in, z_sem)
    far_return.wait()

    for place in range(MOST[0]):
        columns = head_columns(sent_heads[place])
        theirs = masks[2] * (counts[1:2, :] > place).astype(F32).astype(BF16) != 0
        for i in range(2):
            for u in range(TILES):
                window[place % 4, i, tile_rows(my_rows, u), :] = chosen(
                    0, [(case, back_tiles[slot, i]) for case, slot in cases_of_tile(place, u)]
                )
            result[i, :, columns] = jnp.where(theirs, window[place % 4, i], result[i, :, columns])
    sum_ref[...] = total(z_in, copies).reshape(2, HEADS, DEPTH)
    for copy in near_copies + far_copies:
        copy.wait_send()


def hand_out(result, sums, out_q, out_k, sum_q, sum_k, sem):
    copies = [pltpu.make_async_copy(result.at[i], out, sem.at[i]) for i, out in enumerate((out_q, out_k))]
    copies += [pltpu.make_async_copy(sums.at[i], out, sem.at[2 + i]) for i, out in enumerate((sum_q, sum_k))]
    for copy in copies:
        copy.start()
    for copy in copies:
        copy.wait()


def per_device(q_pre, k_pre, values, grad_out, segment_ids, gain_q, gain_k):
    anywhere = pl.BlockSpec(memory_space=pl.ANY)
    vmem, dma = pltpu.VMEM, pltpu.SemaphoreType.DMA
    wide = (ROWS, WIDTH)
    part = (HEADS, DEPTH)
    result, sums = pl.pallas_call(
        kernel,
        out_shape=[vmem((2,) + wide, BF16), vmem((2,) + part, F32)],
        in_specs=[anywhere] * 7,
        out_specs=[pl.BlockSpec(memory_space=vmem)] * 2,
        scratch_shapes=[
            vmem((4,) + wide, BF16),
            vmem((4, ROWS, NEAR_WIDTH), BF16),
            vmem((2, ROWS, NEAR_WIDTH), BF16),
            vmem((2, ROWS, NEAR_WIDTH), BF16),
            vmem((SLOTS, 4, TILE, DEPTH), BF16),
            vmem((SLOTS, 4, TILE, DEPTH), BF16),
            vmem((MOST[0], 2, ROWS, DEPTH), BF16),
            vmem((SLOTS, 2, TILE, DEPTH), BF16),
            vmem((SLOTS, 2, TILE, DEPTH), BF16),
            vmem((2,) + part, F32),
            vmem((2,) + part, F32),
            vmem((1, ROWS), jnp.int32),
            vmem((8, ROWS), jnp.int32),
            vmem((2, 8, ROWS), jnp.int32),
            vmem((3, ROWS, ROWS), F32),
            vmem((3, ROWS, ROWS), F32),
            vmem((4, ROWS, ROWS), BF16),
            vmem((HEADS, 2, ROWS, DEPTH), F32),
            vmem((8, DEPTH), jnp.int32),
            vmem((2, TILES, TILE, DEPTH), BF16),
            vmem((4, 4, ROWS, DEPTH), BF16),
            vmem((2,) + part, F32),
            vmem((4, 2 * HEADS, DEPTH), BF16),
            vmem((8, 2 * HEADS, DEPTH), BF16),
            vmem((8, 2 * HEADS, DEPTH), BF16),
            dma((7,)),
            dma((2,)),
            dma((2,)),
            dma((4, 2)),
            dma((len(PIECES) - 1, 2)),
            dma((2,)),
            dma((2,)),
            dma((2,)),
            dma((2, 4)),
            dma((2, 8)),
            dma((2, 8)),
            pltpu.SemaphoreType.REGULAR,
            pltpu.SemaphoreType.REGULAR,
        ],
        compiler_params=pltpu.CompilerParams(
            collective_id=0, has_side_effects=True, vmem_limit_bytes=56 * 1024 * 1024
        ),
        cost_estimate=pl.CostEstimate(
            flops=HEADS * 8 * 256 * 256 * 128, bytes_accessed=5 << 20, transcendentals=HEADS * 256 * 256
        ),
    )(q_pre[0], k_pre[0], values[0], grad_out[0], segment_ids, gain_q, gain_k)
    out_q, out_k, sum_q, sum_k = pl.pallas_call(
        hand_out,
        out_shape=[
            jax.ShapeDtypeStruct(wide, BF16),
            jax.ShapeDtypeStruct(wide, BF16),
            jax.ShapeDtypeStruct(part, F32),
            jax.ShapeDtypeStruct(part, F32),
        ],
        in_specs=[pl.BlockSpec(memory_space=vmem)] * 2,
        out_specs=[anywhere] * 4,
        scratch_shapes=[dma((4,))],
        compiler_params=pltpu.CompilerParams(vmem_limit_bytes=4 * 1024 * 1024),
    )(result, sums)
    return out_q[None], out_k[None], sum_q, sum_k


def solution(mesh):
    tokens = P("dp", "fsdp", None)
    return jax.shard_map(
        per_device,
        mesh=mesh,
        in_specs=(tokens, tokens, tokens, tokens, P("dp", "fsdp"), P(), P()),
        out_specs=(tokens, tokens, P(), P()),
        check_vma=False,
    )
```
